32 devices in a mesh: blk: 4 (over y, x), clip: 8 (over z, core).
Axes of the slice: x: 2, y: 2, z: 4, core: 2. Of those that a mesh axis runs over, the one named last changes fastest.
Arguments:
- query_rows: bfloat16 [8, 768, 3072], P('clip', 'blk'), may hold values from -5.2 to 5.2
- key_rows: bfloat16 [8, 768, 3072], P('clip', 'blk'), may hold values from -5.2 to 5.2
- value_rows: bfloat16 [8, 768, 3072], P('clip', 'blk'), may hold values from -15 to 15
- residual: bfloat16 [8, 768, 3072], P('clip', 'blk'), may hold values from -12 to 12
- query_tangent: bfloat16 [8, 768, 3072], P(None, ('blk', 'clip')), may hold values from -6 to 6
- key_tangent: bfloat16 [8, 768, 3072], P(None, ('blk', 'clip')), may hold values from -6 to 6
- value_tangent: bfloat16 [8, 768, 3072], P(None, ('blk', 'clip')), may hold values from -15 to 15
- velocity: bfloat16 [8, 768, 3072], P(None, ('blk', 'clip')), may hold values from -12 to 12
- clip_slot: int32 [8], replicated, may hold values from 0 to 7, each once
- token_slot: int32 [32, 24], P(('blk', 'clip')), may hold values from 0 to 23, each once within a row
- clip_time: float32 [8], P('clip'), may hold values from 0.2 to 1.4
Outputs:
- attention_out: bfloat16 [8, 768, 3072], P('clip', 'blk')
- attention_tangent: bfloat16 [8, 768, 3072], P('clip', 'blk')
- target: bfloat16 [8, 768, 3072], P('clip', 'blk')
The draws below stay inside these ranges and needn't reach their ends.
Inputs may be any that keep to these rules, and one draw needn't show every extreme that they name: `clip_slot`: a permutation: every clip has one teacher row. `token_slot`: every row is a permutation of the 24 positions of its run.
All inputs are finite; a program needn't handle non-finite values.
Results may differ from the reference program's by a relative error of at most 0.02.
Values may be sent and summed in bfloat16 or wider, within the bound.
A program may use at most 256 MiB of HBM per device.

```python
import jax
import jax.numpy as jnp
from jax import lax

HEAD_DIM = 128
HEADS = 24
WIDTH = 3072
CLIPS = 8
SEQ = 768
PIECE = 24
N_BLK = 4
N_CLIP = 8


def draw_query_rows(key, part):
    key = jax.random.fold_in(key, 1)
    bulk = jnp.clip(1.3 * jax.random.normal(key, (CLIPS, SEQ, WIDTH), jnp.float32), -5.2, 5.2)
    return bulk.astype(jnp.bfloat16)


def draw_key_rows(key, part):
    key = jax.random.fold_in(key, 2)
    bulk = jnp.clip(1.3 * jax.random.normal(key, (CLIPS, SEQ, WIDTH), jnp.float32), -5.2, 5.2)
    return bulk.astype(jnp.bfloat16)


def rising_rows(key, low_rise):
    position = jnp.arange(SEQ, dtype=jnp.float32) / (SEQ - 1)
    bulk = jnp.clip(jax.random.normal(key, (CLIPS, SEQ, WIDTH), jnp.float32), -4.0, 4.0)
    rise = 1.0 + low_rise * position
    return (bulk * rise[None, :, None]).astype(jnp.bfloat16)


def draw_residual(key, part):
    key = jax.random.fold_in(key, 3)
    return rising_rows(key, 2.0)


def draw_velocity(key, part):
    key = jax.random.fold_in(key, 4)
    return rising_rows(key, 2.0)


def levels(key, dims, cuts, least, top_value):
    def one(axis_at, shards_of):
        draws = jax.random.uniform(jax.random.fold_in(jax.random.fold_in(key, 6), axis_at), (shards_of,), jnp.float32, least / len(cuts), top_value / len(cuts))
        return jnp.repeat(jnp.exp(draws), dims[axis_at] // shards_of).reshape((-1,) + (1,) * (len(dims) - axis_at - 1))

    loudness = one(*cuts[0])
    for cut in cuts[1:]:
        loudness = loudness * one(*cut)
    return loudness


def noise(key, dims, width, reach, shards=(), kind=jnp.bfloat16):
    array = jax.random.normal(key, dims, jnp.float32) * width
    if len(shards) > 0:
        array = levels(key, dims, shards, -0.22, 0.18) * array
    return jnp.clip(array, min=-reach, max=reach).astype(kind)


def setup_inputs(seed: int = 0) -> dict:
    keys = jax.random.split(jax.random.key(seed), 12)
    query_rows = draw_query_rows(jax.random.fold_in(keys[11], 71), 0)
    key_rows = draw_key_rows(jax.random.fold_in(keys[11], 71), 0)
    value_rows = noise(keys[2], (CLIPS, SEQ, WIDTH), 3.0, 15.0, ((0, 8), (1, 4)))
    residual = draw_residual(jax.random.fold_in(keys[11], 71), 0)
    query_tangent = noise(keys[4], (CLIPS, SEQ, WIDTH), 1.0, 6.0, ((1, 32),))
    key_tangent = noise(keys[5], (CLIPS, SEQ, WIDTH), 1.0, 6.0, ((1, 32),))
    value_tangent = noise(keys[6], (CLIPS, SEQ, WIDTH), 3.0, 15.0, ((1, 32),))
    velocity = draw_velocity(jax.random.fold_in(keys[11], 71), 0)
    clip_slot = jax.random.permutation(keys[8], CLIPS).astype(jnp.int32)
    token_slot = jax.vmap(lambda own: jax.random.permutation(own, PIECE))(jax.random.split(keys[9], (N_BLK * N_CLIP))).reshape((N_BLK * N_CLIP, PIECE)).astype(jnp.int32)
    clip_time = jnp.clip(0.2 + 1.19999997 * jax.random.uniform(keys[10], (CLIPS,), jnp.float32) ** levels(keys[10], (CLIPS,), ((0, 8),), -0.2, 0.2), 0.2, 1.4)
    return dict(query_rows=query_rows, key_rows=key_rows, value_rows=value_rows, residual=residual, query_tangent=query_tangent, key_tangent=key_tangent, value_tangent=value_tangent, velocity=velocity, clip_slot=clip_slot, token_slot=token_slot, clip_time=clip_time)


sigma_data = 0.5
norm_offset = 0.1

def head_attention(operands):
    query_head, key_head, value_head, query_dot, key_dot, value_dot = operands
    score_scale = HEAD_DIM ** (-0.5)
    scores = jnp.dot(query_head, key_head.T, preferred_element_type=jnp.float32) * score_scale
    score_dot = (jnp.dot(query_dot, key_head.T, preferred_element_type=jnp.float32) + jnp.dot(query_head, key_dot.T, preferred_element_type=jnp.float32)) * score_scale
    row_max = lax.optimization_barrier(jnp.max(scores, axis=1, keepdims=True))
    weights = jnp.exp(scores - row_max)
    row_total = lax.optimization_barrier(jnp.sum(weights, axis=1, keepdims=True))
    weighted = weights * score_dot
    dot_total = lax.optimization_barrier(jnp.sum(weighted, axis=1, keepdims=True))
    weights_low = weights.astype(jnp.bfloat16)
    weighted_low = weighted.astype(jnp.bfloat16)
    mixed = jnp.dot(weights_low, value_head, preferred_element_type=jnp.float32)
    mixed_dot = jnp.dot(weights_low, value_dot, preferred_element_type=jnp.float32)
    carried = jnp.dot(weighted_low, value_head, preferred_element_type=jnp.float32)
    attention = mixed / row_total
    tangent = (carried + mixed_dot) / row_total - dot_total / row_total * attention
    return (attention.astype(jnp.bfloat16), tangent.astype(jnp.bfloat16))

def student_order(teacher, clip_slot, token_slot):
    run_length = token_slot.shape[1]
    starts = jnp.arange(token_slot.shape[0], dtype=jnp.int32)[:, None] * run_length
    positions = (starts + token_slot).reshape(-1).astype(jnp.int32)
    by_clip = jnp.take(teacher, clip_slot.astype(jnp.int32), axis=0)
    return jnp.take(by_clip, positions, axis=1)

def split_heads(feature_rows):
    return feature_rows.reshape(SEQ, HEADS, HEAD_DIM).transpose(1, 0, 2)

def merge_heads(head_rows):
    return head_rows.transpose(1, 0, 2).reshape(SEQ, WIDTH)

def clip_block(operands):
    heads = tuple((split_heads(feature_rows) for feature_rows in operands))
    attention, tangent = lax.map(head_attention, heads)
    return (merge_heads(attention), merge_heads(tangent))

def reference(query_rows, key_rows, value_rows, residual, query_tangent, key_tangent, value_tangent, velocity, clip_slot, token_slot, clip_time):
    query_dot = student_order(query_tangent, clip_slot, token_slot)
    key_dot = student_order(key_tangent, clip_slot, token_slot)
    value_dot = student_order(value_tangent, clip_slot, token_slot)
    velocity_rows = student_order(velocity, clip_slot, token_slot)
    attention_out, attention_tangent = lax.map(clip_block, (query_rows, key_rows, value_rows, query_dot, key_dot, value_dot))
    cosine = jnp.cos(clip_time)[:, None, None]
    sine = jnp.sin(clip_time)[:, None, None]
    mismatch = -cosine * cosine * (sigma_data * attention_out.astype(jnp.float32) - velocity_rows.astype(jnp.float32)) - cosine * sine * (residual.astype(jnp.float32) + sigma_data * attention_tangent.astype(jnp.float32))
    mean_square = lax.optimization_barrier(jnp.sum(mismatch * mismatch, axis=(1, 2), keepdims=True)) / (SEQ * WIDTH)
    target = (mismatch / (jnp.sqrt(mean_square) + norm_offset)).astype(jnp.bfloat16)
    return (attention_out, attention_tangent, target)
```

```python
import functools
import math

import jax
import jax.numpy as jnp
from jax import lax
from jax.experimental import pallas as pl
from jax.experimental.pallas import tpu as pltpu
from jax.sharding import PartitionSpec as P

HEAD_DIM = 128
SIGMA = 0.5
OFFSET = 0.1
MESH = pl.DeviceIdType.MESH
F32 = jnp.float32
BF16 = jnp.bfloat16


def kernel(
    nb, nc, hc, chunks,
    slot_ref, coef_ref, pick_ref,
    q_ref, k_ref, v_ref, res_ref,
    qt_ref, kt_ref, vt_ref, vel_ref,
    out_ref, tan_ref, target_ref,
    teach, teach_vel, send, recv, stud, dots, own_out, got_out, vel_send, vel_recv, resid, mism, goal,
    part, parts,
    load_sem, send_sem, recv_sem, stud_send, stud_recv, out_send, out_recv,
    vel_ssem, vel_rsem, part_send, part_recv, write_sem,
):
    n = nb * nc
    run = teach.shape[2]
    tok = q_ref.shape[1]
    width = q_ref.shape[2]
    seq = stud.shape[1]
    group_width = width // nb
    cw = hc * HEAD_DIM
    join = 16 // math.gcd(run, 16)
    my_b = lax.axis_index("blk")
    my_c = lax.axis_index("clip")
    me = my_b * nc + my_c

    loads = []
    for t, ref in enumerate((qt_ref, kt_ref, vt_ref)):
        loads.append(pltpu.make_async_copy(ref, teach.at[t], load_sem.at[t]))
    loads.append(pltpu.make_async_copy(vel_ref, teach_vel, load_sem.at[3]))
    loads.append(pltpu.make_async_copy(res_ref.at[0], resid, load_sem.at[4]))
    for load in loads:
        load.start()

    barrier = pltpu.get_barrier_semaphore()

    @pl.loop(1, n)
    def _(m):
        d = lax.rem(me + m, n)
        pl.semaphore_signal(barrier, inc=1, device_id=(d // nc, lax.rem(d, nc)), device_id_type=MESH)

    pick = pick_ref[...]

    def build(c, d):
        g, i = d // nc, lax.rem(d, nc)
        slot = slot_ref[i]
        col = pl.multiple_of(g * group_width + c * cw, 128)
        pieces = []
        for t in range(3):
            rows = jnp.dot(pick, teach[t, slot, :, pl.ds(col, cw)], preferred_element_type=F32)
            for hh in range(hc):
                pieces.append(rows[:, hh * HEAD_DIM:(hh + 1) * HEAD_DIM])
        spare = send.shape[2] - 3 * hc * run
        if spare:
            pieces.append(jnp.zeros((spare, HEAD_DIM), F32))
        send[c, d] = jnp.concatenate(pieces, axis=0).astype(BF16)

    def students(c):
        for s, ref in enumerate((q_ref, k_ref, v_ref)):
            for off in range(nb):
                g = lax.rem(my_b + off, nb)
                src = ref.at[0, :, pl.ds(pl.multiple_of(g * group_width + c * cw, 128), cw)]
                dst = stud.at[s, pl.ds(pl.multiple_of(my_b * tok, 16), tok), pl.ds(c * cw, cw)]
                if off == 0:
                    pltpu.make_async_copy(src, dst, stud_recv.at[c]).start()
                else:
                    pltpu.make_async_remote_copy(
                        src_ref=src, dst_ref=dst, send_sem=stud_send, recv_sem=stud_recv.at[c],
                        device_id=(g, my_c), device_id_type=MESH,
                    ).start()

    for load in loads[:3]:
        load.wait()
    pl.semaphore_wait(barrier, n - 1)

    for c in range(chunks):
        @pl.loop(1, n)
        def _(m):
            d = lax.rem(me + m, n)
            build(c, d)
            pltpu.make_async_remote_copy(
                src_ref=send.at[c, d], dst_ref=recv.at[c, me],
                send_sem=send_sem, recv_sem=recv_sem.at[c],
                device_id=(d // nc, lax.rem(d, nc)), device_id_type=MESH,
            ).start()

        build(c, me)
        pltpu.make_async_copy(send.at[c, me], recv.at[c, me], recv_sem.at[c]).start()
        students(c)

    loads[3].wait()

    def build_velocity(i):
        slot = slot_ref[i]
        rows = jnp.dot(pick, teach_vel[slot], preferred_element_type=F32)
        heads = [rows[:, h * HEAD_DIM:(h + 1) * HEAD_DIM] for h in range(width // HEAD_DIM)]
        vel_send[i] = jnp.concatenate(heads, axis=0).astype(BF16)

    @pl.loop(1, nc)
    def _(m):
        i = lax.rem(my_c + m, nc)
        build_velocity(i)
        pltpu.make_async_remote_copy(
            src_ref=vel_send.at[i], dst_ref=vel_recv.at[my_c],
            send_sem=vel_ssem, recv_sem=vel_rsem,
            device_id=(my_b, i), device_id_type=MESH,
        ).start()

    build_velocity(my_c)
    pltpu.make_async_copy(vel_send.at[my_c], vel_recv.at[my_c], vel_rsem).start()

    scale = HEAD_DIM ** (-0.5)
    tile = 256
    for c in range(chunks):
        pltpu.make_async_copy(recv.at[c], recv.at[c], recv_sem.at[c]).wait()
        waited = stud.at[:, :, pl.ds(c * cw, cw)]
        pltpu.make_async_copy(waited, waited, stud_recv.at[c]).wait()

        @pl.loop(0, n // join)
        def _(j):
            slabs = [recv[c, j * join + u].astype(F32) for u in range(join)]
            for t in range(3):
                for hh in range(hc):
                    at = (t * hc + hh) * run
                    rows = jnp.concatenate([slab[at:at + run] for slab in slabs], axis=0)
                    dots[t, hh, pl.ds(pl.multiple_of(j * (join * run), 16), join * run), :] = rows.astype(BF16)

        for hh in range(hc):
            lane = c * cw + hh * HEAD_DIM

            @pl.loop(0, seq // tile)
            def _(r):
                at = pl.ds(pl.multiple_of(r * tile, tile), tile)
                keys = stud[1, :, lane:lane + HEAD_DIM]
                both_keys = jnp.concatenate([keys, dots[1, hh]], axis=1)
                both_values = jnp.concatenate([stud[2, :, lane:lane + HEAD_DIM], dots[2, hh]], axis=1)
                query = stud[0, at, lane:lane + HEAD_DIM]
                both_queries = jnp.concatenate([dots[0, hh, at, :], query], axis=1)
                over = (((1,), (1,)), ((), ()))
                scores = lax.dot_general(query, keys, over, preferred_element_type=F32)
                score_dot = lax.dot_general(both_queries, both_keys, over, preferred_element_type=F32)
                top = jnp.max(scores, axis=1, keepdims=True)
                weights = jnp.exp2((scores - top) * (scale * math.log2(math.e)))
                weighted = weights * score_dot
                total = jnp.sum(weights, axis=1, keepdims=True)
                dot_total = jnp.sum(weighted, axis=1, keepdims=True) * scale
                mixed = jnp.dot(weights.astype(BF16), both_values, preferred_element_type=F32)
                carried = jnp.dot(
                    weighted.astype(BF16), both_values[:, :HEAD_DIM], preferred_element_type=F32
                )
                inverse = 1.0 / total
                attention = mixed[:, :HEAD_DIM] * inverse
                tangent = (carried * scale + mixed[:, HEAD_DIM:]) * inverse - (dot_total * inverse) * attention
                own_out[0, at, lane:lane + HEAD_DIM] = attention.astype(BF16)
                own_out[1, at, lane:lane + HEAD_DIM] = tangent.astype(BF16)

        for off in [*range(1, nb), 0]:
            b = lax.rem(my_b + off, nb)
            src = own_out.at[:, pl.ds(pl.multiple_of(b * tok, 16), tok), pl.ds(c * cw, cw)]
            dst = got_out.at[:, :, pl.ds(pl.multiple_of(my_b * group_width + c * cw, 128), cw)]
            if off == 0:
                pltpu.make_async_copy(src, dst, out_recv.at[c]).start()
            else:
                pltpu.make_async_remote_copy(
                    src_ref=src, dst_ref=dst, send_sem=out_send, recv_sem=out_recv.at[c],
                    device_id=(b, my_c), device_id_type=MESH,
                ).start()

    pltpu.make_async_copy(vel_recv, vel_recv, vel_rsem).wait()
    loads[4].wait()
    for c in range(chunks):
        waited = got_out.at[:, :, pl.ds(0, nb * cw)]
        pltpu.make_async_copy(waited, waited, out_recv.at[c]).wait()
    writes = [
        pltpu.make_async_copy(got_out.at[0], out_ref.at[0], write_sem.at[0]),
        pltpu.make_async_copy(got_out.at[1], tan_ref.at[0], write_sem.at[1]),
    ]
    for write in writes:
        write.start()

    square_cos, cos_sin = coef_ref[0], coef_ref[1]
    part[...] = jnp.zeros_like(part)

    @pl.loop(0, width // HEAD_DIM // join)
    def _(j):
        blocks = [
            vel_recv[p, pl.ds(pl.multiple_of(j * (join * run), 16), join * run), :].astype(F32)
            for p in range(nc)
        ]
        added = part[...]
        for u in range(join):
            at = pl.ds(pl.multiple_of((j * join + u) * HEAD_DIM, 128), HEAD_DIM)
            velocity = jnp.concatenate([block[u * run:(u + 1) * run] for block in blocks], axis=0)
            off = -square_cos * (SIGMA * got_out[0, :, at].astype(F32) - velocity) - cos_sin * (
                resid[:, at].astype(F32) + SIGMA * got_out[1, :, at].astype(F32)
            )
            mism[:, at] = off
            added = added + jnp.sum((off * off).reshape(tok // 8, 8, HEAD_DIM), axis=0)
        part[...] = added

    for off in range(1, nb):
        pltpu.make_async_remote_copy(
            src_ref=part, dst_ref=parts.at[off - 1], send_sem=part_send, recv_sem=part_recv,
            device_id=(lax.rem(my_b + off, nb), my_c), device_id_type=MESH,
        ).start()
    pltpu.make_async_copy(parts, parts, part_recv).wait()
    whole = part[...] + jnp.sum(parts[...], axis=0)
    mean_square = jnp.sum(whole, keepdims=True) / (nb * tok * width)
    factor = 1.0 / (jnp.sqrt(mean_square) + OFFSET)

    @pl.loop(0, width // HEAD_DIM)
    def _(h):
        at = pl.ds(pl.multiple_of(h * HEAD_DIM, 128), HEAD_DIM)
        goal[:, at] = (mism[:, at] * factor).astype(BF16)

    last = pltpu.make_async_copy(goal, target_ref.at[0], write_sem.at[2])
    last.start()

    pltpu.make_async_copy(parts, parts, part_send).wait()
    sent = recv.at[:, pl.ds(0, n - 1)]
    pltpu.make_async_copy(sent, sent, send_sem).wait()
    sent = stud.at[:, pl.ds(0, (nb - 1) * tok), :]
    pltpu.make_async_copy(sent, sent, stud_send).wait()
    sent = got_out.at[:, :, pl.ds(0, (nb - 1) * group_width)]
    pltpu.make_async_copy(sent, sent, out_send).wait()
    sent = vel_recv.at[pl.ds(0, nc - 1)]
    pltpu.make_async_copy(sent, sent, vel_ssem).wait()
    for write in writes:
        write.wait()
    last.wait()


def local(
    nb, nc,
    query_rows, key_rows, value_rows, residual,
    query_tangent, key_tangent, value_tangent, velocity,
    clip_slot, token_slot, clip_time,
):
    _, tok, width = query_rows.shape
    clips, run, _ = query_tangent.shape
    n = nb * nc
    seq = nb * tok
    own_heads = width // HEAD_DIM // nb
    hc = 2 if own_heads % 2 == 0 else 1
    chunks = own_heads // hc
    slab = -(-3 * hc * run // 16) * 16
    group_width = width // nb
    heads = width // HEAD_DIM
    cosine, sine = jnp.cos(clip_time[0]), jnp.sin(clip_time[0])
    coef = jnp.stack([cosine * cosine, cosine * sine])
    pick = (token_slot[0][:, None] == jnp.arange(run, dtype=jnp.int32)[None, :]).astype(BF16)
    out = jax.ShapeDtypeStruct((1, tok, width), BF16)
    anywhere = pl.BlockSpec(memory_space=pl.ANY)
    small = pl.BlockSpec(memory_space=pltpu.SMEM)
    dma = pltpu.SemaphoreType.DMA
    return pl.pallas_call(
        functools.partial(kernel, nb, nc, hc, chunks),
        out_shape=(out, out, out),
        in_specs=[small, small, pl.BlockSpec(memory_space=pltpu.VMEM)] + [anywhere] * 8,
        out_specs=(anywhere,) * 3,
        scratch_shapes=[
            pltpu.VMEM((3, clips, run, width), BF16),
            pltpu.VMEM((clips, run, width), BF16),
            pltpu.VMEM((chunks, n, slab, HEAD_DIM), BF16),
            pltpu.VMEM((chunks, n, slab, HEAD_DIM), BF16),
            pltpu.VMEM((3, seq, group_width), BF16),
            pltpu.VMEM((3, hc, seq, HEAD_DIM), BF16),
            pltpu.VMEM((2, seq, group_width), BF16),
            pltpu.VMEM((2, tok, width), BF16),
            pltpu.VMEM((nc, heads * run, HEAD_DIM), BF16),
            pltpu.VMEM((nc, heads * run, HEAD_DIM), BF16),
            pltpu.VMEM((tok, width), BF16),
            pltpu.VMEM((tok, width), F32),
            pltpu.VMEM((tok, width), BF16),
            pltpu.VMEM((8, HEAD_DIM), F32),
            pltpu.VMEM((nb - 1, 8, HEAD_DIM), F32),
            dma((5,)), dma, dma((chunks,)), dma, dma((chunks,)), dma, dma((chunks,)),
            dma, dma, dma, dma, dma((3,)),
        ],
        compiler_params=pltpu.CompilerParams(
            collective_id=0, has_side_effects=True, vmem_limit_bytes=56 * 1024 * 1024
        ),
        name="clip_attention",
    )(
        clip_slot, coef, pick,
        query_rows, key_rows, value_rows, residual,
        query_tangent, key_tangent, value_tangent, velocity,
    )


def solution(mesh):
    rows = P("clip", "blk", None)
    teacher = P(None, ("blk", "clip"), None)
    in_specs = (rows,) * 4 + (teacher,) * 4 + (P(), P(("blk", "clip"), None), P("clip"))
    return jax.shard_map(
        functools.partial(local, mesh.shape["blk"], mesh.shape["clip"]),
        mesh=mesh, in_specs=in_specs, out_specs=(rows,) * 3, check_vma=False,
    )
```

```python
import functools
import math

import jax
import jax.numpy as jnp
from jax import lax
from jax.experimental import pallas as pl
from jax.experimental.pallas import tpu as pltpu
from jax.sharding import PartitionSpec as P

HEAD_DIM = 128
SIGMA = 0.5
OFFSET = 0.1
MESH = pl.DeviceIdType.MESH
F32 = jnp.float32
BF16 = jnp.bfloat16


def kernel(
    nb, nc, hc, chunks,
    slot_ref, token_ref, time_ref,
    q_ref, k_ref, v_ref, res_ref,
    qt_ref, kt_ref, vt_ref, vel_ref,
    both_ref, mism_ref, factor_ref,
    teach, teach_vel, send, recv, stud, dots, own_out, got_out, vel_send, vel_recv, resid, mism, picks,
    part, parts,
    load_sem, send_sem, recv_sem, stud_send, stud_recv, out_send, out_recv,
    vel_ssem, vel_rsem, part_send, part_recv, write_sem,
):
    n = nb * nc
    run = teach.shape[2]
    tok = q_ref.shape[1]
    width = q_ref.shape[2]
    seq = stud.shape[1]
    group_width = width // nb
    cw = hc * HEAD_DIM
    join = 16 // math.gcd(run, 16)
    my_b = lax.axis_index("blk")
    my_c = lax.axis_index("clip")
    me = my_b * nc + my_c

    loads = []
    for t, ref in enumerate((qt_ref, kt_ref, vt_ref)):
        loads.append(pltpu.make_async_copy(ref, teach.at[t], load_sem.at[t]))
    loads.append(pltpu.make_async_copy(vel_ref, teach_vel, load_sem.at[3]))
    loads.append(pltpu.make_async_copy(res_ref.at[0], resid, load_sem.at[4]))
    for load in loads:
        load.start()

    barrier = pltpu.get_barrier_semaphore()

    @pl.loop(1, n)
    def _(m):
        d = lax.rem(me + m, n)
        pl.semaphore_signal(barrier, inc=1, device_id=(d // nc, lax.rem(d, nc)), device_id_type=MESH)

    place = lax.broadcasted_iota(jnp.int32, (1, run), 1)
    for r in range(run):
        picks[r:r + 1, :] = (place == token_ref[0, r]).astype(F32)
    pick = picks[...].astype(BF16)
    time = jnp.full((1, HEAD_DIM), time_ref[0], F32)
    cosine, sine = jnp.cos(time), jnp.sin(time)

    def build(c, d):
        g, i = d // nc, lax.rem(d, nc)
        slot = slot_ref[i]
        col = pl.multiple_of(g * group_width + c * cw, 128)
        pieces = []
        for t in range(3):
            rows = jnp.dot(pick, teach[t, slot, :, pl.ds(col, cw)], preferred_element_type=F32)
            for hh in range(hc):
                pieces.append(rows[:, hh * HEAD_DIM:(hh + 1) * HEAD_DIM])
        spare = send.shape[2] - 3 * hc * run
        if spare:
            pieces.append(jnp.zeros((spare, HEAD_DIM), F32))
        send[c, d] = jnp.concatenate(pieces, axis=0).astype(BF16)

    def students(c):
        for s, ref in enumerate((q_ref, k_ref, v_ref)):
            for off in range(nb):
                g = lax.rem(my_b + off, nb)
                src = ref.at[0, :, pl.ds(pl.multiple_of(g * group_width + c * cw, 128), cw)]
                dst = stud.at[s, pl.ds(pl.multiple_of(my_b * tok, 16), tok), pl.ds(c * cw, cw)]
                if off == 0:
                    pltpu.make_async_copy(src, dst, stud_recv.at[c]).start()
                else:
                    pltpu.make_async_remote_copy(
                        src_ref=src, dst_ref=dst, send_sem=stud_send, recv_sem=stud_recv.at[c],
                        device_id=(g, my_c), device_id_type=MESH,
                    ).start()

    for load in loads[:3]:
        load.wait()
    pl.semaphore_wait(barrier, n - 1)

    for c in range(chunks):
        @pl.loop(1, n)
        def _(m):
            d = lax.rem(my_b + lax.rem(m, nb), nb) * nc + lax.rem(my_c + lax.rem(m // nb * 3, nc), nc)
            build(c, d)
            pltpu.make_async_remote_copy(
                src_ref=send.at[c, d], dst_ref=recv.at[c, me],
                send_sem=send_sem, recv_sem=recv_sem.at[c],
                device_id=(d // nc, lax.rem(d, nc)), device_id_type=MESH,
            ).start()

        build(c, me)
        pltpu.make_async_copy(send.at[c, me], recv.at[c, me], recv_sem.at[c]).start()
        students(c)

    loads[3].wait()

    def build_velocity(i):
        slot = slot_ref[i]
        rows = jnp.dot(pick, teach_vel[slot], preferred_element_type=F32)
        heads = [rows[:, h * HEAD_DIM:(h + 1) * HEAD_DIM] for h in range(width // HEAD_DIM)]
        vel_send[i] = jnp.concatenate(heads, axis=0).astype(BF16)

    @pl.loop(1, nc)
    def _(m):
        i = lax.rem(my_c + m, nc)
        build_velocity(i)
        pltpu.make_async_remote_copy(
            src_ref=vel_send.at[i], dst_ref=vel_recv.at[my_c],
            send_sem=vel_ssem, recv_sem=vel_rsem,
            device_id=(my_b, i), device_id_type=MESH,
        ).start()

    build_velocity(my_c)
    pltpu.make_async_copy(vel_send.at[my_c], vel_recv.at[my_c], vel_rsem).start()

    scale = HEAD_DIM ** (-0.5)
    tile = 256
    for c in range(chunks):
        pltpu.make_async_copy(recv.at[c], recv.at[c], recv_sem.at[c]).wait()
        waited = stud.at[:, :, pl.ds(c * cw, cw)]
        pltpu.make_async_copy(waited, waited, stud_recv.at[c]).wait()

        @pl.loop(0, n // join)
        def _(j):
            slabs = [recv[c, j * join + u].astype(F32) for u in range(join)]
            for t in range(3):
                for hh in range(hc):
                    at = (t * hc + hh) * run
                    rows = jnp.concatenate([slab[at:at + run] for slab in slabs], axis=0)
                    dots[t, hh, pl.ds(pl.multiple_of(j * (join * run), 16), join * run), :] = rows.astype(BF16)

        for hh in range(hc):
            lane = c * cw + hh * HEAD_DIM

            @pl.loop(0, seq // tile)
            def _(r):
                at = pl.ds(pl.multiple_of(r * tile, tile), tile)
                keys = stud[1, :, lane:lane + HEAD_DIM]
                both_keys = jnp.concatenate([keys, dots[1, hh]], axis=1)
                both_values = jnp.concatenate([stud[2, :, lane:lane + HEAD_DIM], dots[2, hh]], axis=1)
                query = stud[0, at, lane:lane + HEAD_DIM]
                both_queries = jnp.concatenate([dots[0, hh, at, :], query], axis=1)
                over = (((1,), (1,)), ((), ()))
                scores = lax.dot_general(query, keys, over, preferred_element_type=F32)
                score_dot = lax.dot_general(both_queries, both_keys, over, preferred_element_type=F32)
                top = jnp.max(scores, axis=1, keepdims=True)
                weights = jnp.exp2((scores - top) * (scale * math.log2(math.e)))
                weighted = weights * score_dot
                total = jnp.sum(weights, axis=1, keepdims=True)
                dot_total = jnp.sum(weighted, axis=1, keepdims=True) * scale
                mixed = jnp.dot(weights.astype(BF16), both_values, preferred_element_type=F32)
                carried = jnp.dot(
                    weighted.astype(BF16), both_values[:, :HEAD_DIM], preferred_element_type=F32
                )
                inverse = 1.0 / total
                attention = mixed[:, :HEAD_DIM] * inverse
                tangent = (carried * scale + mixed[:, HEAD_DIM:]) * inverse - (dot_total * inverse) * attention
                own_out[0, at, lane:lane + HEAD_DIM] = attention.astype(BF16)
                own_out[1, at, lane:lane + HEAD_DIM] = tangent.astype(BF16)

        for off in [*range(1, nb), 0]:
            b = lax.rem(my_b + off, nb)
            src = own_out.at[:, pl.ds(pl.multiple_of(b * tok, 16), tok), pl.ds(c * cw, cw)]
            dst = got_out.at[:, :, pl.ds(pl.multiple_of(my_b * group_width + c * cw, 128), cw)]
            if off == 0:
                pltpu.make_async_copy(src, dst, out_recv.at[c]).start()
            else:
                pltpu.make_async_remote_copy(
                    src_ref=src, dst_ref=dst, send_sem=out_send, recv_sem=out_recv.at[c],
                    device_id=(b, my_c), device_id_type=MESH,
                ).start()

    pltpu.make_async_copy(vel_recv, vel_recv, vel_rsem).wait()
    loads[4].wait()
    for c in range(chunks):
        waited = got_out.at[:, :, pl.ds(0, nb * cw)]
        pltpu.make_async_copy(waited, waited, out_recv.at[c]).wait()
    writes = [
        pltpu.make_async_copy(got_out, both_ref, write_sem.at[0]),
        pltpu.make_async_copy(mism, mism_ref, write_sem.at[1]),
    ]
    writes[0].start()

    square_cos, cos_sin = cosine * cosine, cosine * sine
    part[...] = jnp.zeros_like(part)

    @pl.loop(0, width // HEAD_DIM // join)
    def _(j):
        blocks = [
            vel_recv[p, pl.ds(pl.multiple_of(j * (join * run), 16), join * run), :].astype(F32)
            for p in range(nc)
        ]
        added = part[...]
        for u in range(join):
            at = pl.ds(pl.multiple_of((j * join + u) * HEAD_DIM, 128), HEAD_DIM)
            velocity = jnp.concatenate([block[u * run:(u + 1) * run] for block in blocks], axis=0)
            off = -square_cos * (SIGMA * got_out[0, :, at].astype(F32) - velocity) - cos_sin * (
                resid[:, at].astype(F32) + SIGMA * got_out[1, :, at].astype(F32)
            )
            mism[:, at] = off
            added = added + jnp.sum((off * off).reshape(tok // 8, 8, HEAD_DIM), axis=0)
        part[...] = added

    for off in range(1, nb):
        pltpu.make_async_remote_copy(
            src_ref=part, dst_ref=parts.at[off - 1], send_sem=part_send, recv_sem=part_recv,
            device_id=(lax.rem(my_b + off, nb), my_c), device_id_type=MESH,
        ).start()
    writes[1].start()
    pltpu.make_async_copy(parts, parts, part_recv).wait()
    whole = part[...] + jnp.sum(parts[...], axis=0)
    mean_square = jnp.sum(whole, keepdims=True) / (nb * tok * width)
    factor_ref[...] = jnp.broadcast_to(1.0 / (jnp.sqrt(mean_square) + OFFSET), factor_ref.shape)

    pltpu.make_async_copy(parts, parts, part_send).wait()
    sent = recv.at[:, pl.ds(0, n - 1)]
    pltpu.make_async_copy(sent, sent, send_sem).wait()
    sent = stud.at[:, pl.ds(0, (nb - 1) * tok), :]
    pltpu.make_async_copy(sent, sent, stud_send).wait()
    sent = got_out.at[:, :, pl.ds(0, (nb - 1) * group_width)]
    pltpu.make_async_copy(sent, sent, out_send).wait()
    sent = vel_recv.at[pl.ds(0, nc - 1)]
    pltpu.make_async_copy(sent, sent, vel_ssem).wait()
    for write in writes:
        write.wait()


def finish(both_ref, mism_ref, factor_ref, out_ref, tan_ref, target_ref):
    out_ref[0] = both_ref[0]
    tan_ref[0] = both_ref[1]
    target_ref[0] = (mism_ref[...] * factor_ref[0:1, 0:1]).astype(BF16)


def local(
    nb, nc,
    query_rows, key_rows, value_rows, residual,
    query_tangent, key_tangent, value_tangent, velocity,
    clip_slot, token_slot, clip_time,
):
    _, tok, width = query_rows.shape
    clips, run, _ = query_tangent.shape
    n = nb * nc
    seq = nb * tok
    own_heads = width // HEAD_DIM // nb
    hc = 2 if own_heads % 2 == 0 else 1
    chunks = own_heads // hc
    slab = -(-3 * hc * run // 16) * 16
    group_width = width // nb
    heads = width // HEAD_DIM
    out = jax.ShapeDtypeStruct((1, tok, width), BF16)
    anywhere = pl.BlockSpec(memory_space=pl.ANY)
    small = pl.BlockSpec(memory_space=pltpu.SMEM)
    dma = pltpu.SemaphoreType.DMA
    both, mism, factor = pl.pallas_call(
        functools.partial(kernel, nb, nc, hc, chunks),
        out_shape=(
            jax.ShapeDtypeStruct((2, tok, width), BF16),
            jax.ShapeDtypeStruct((tok, width), F32),
            jax.ShapeDtypeStruct((8, HEAD_DIM), F32),
        ),
        in_specs=[small] * 3 + [anywhere] * 8,
        out_specs=(anywhere, anywhere, pl.BlockSpec(memory_space=pltpu.VMEM)),
        scratch_shapes=[
            pltpu.VMEM((3, clips, run, width), BF16),
            pltpu.VMEM((clips, run, width), BF16),
            pltpu.VMEM((chunks, n, slab, HEAD_DIM), BF16),
            pltpu.VMEM((chunks, n, slab, HEAD_DIM), BF16),
            pltpu.VMEM((3, seq, group_width), BF16),
            pltpu.VMEM((3, hc, seq, HEAD_DIM), BF16),
            pltpu.VMEM((2, seq, group_width), BF16),
            pltpu.VMEM((2, tok, width), BF16),
            pltpu.VMEM((nc, heads * run, HEAD_DIM), BF16),
            pltpu.VMEM((nc, heads * run, HEAD_DIM), BF16),
            pltpu.VMEM((tok, width), BF16),
            pltpu.VMEM((tok, width), F32),
            pltpu.VMEM((run, run), F32),
            pltpu.VMEM((8, HEAD_DIM), F32),
            pltpu.VMEM((nb - 1, 8, HEAD_DIM), F32),
            dma((5,)), dma, dma((chunks,)), dma, dma((chunks,)), dma, dma((chunks,)),
            dma, dma, dma, dma, dma((2,)),
        ],
        compiler_params=pltpu.CompilerParams(
            collective_id=0, has_side_effects=True, vmem_limit_bytes=56 * 1024 * 1024
        ),
        name="clip_attention",
    )(
        clip_slot, token_slot, clip_time,
        query_rows, key_rows, value_rows, residual,
        query_tangent, key_tangent, value_tangent, velocity,
    )
    step = tok // 2
    row_block = pl.BlockSpec((1, step, width), lambda r: (0, r, 0))
    return pl.pallas_call(
        finish,
        grid=(tok // step,),
        out_shape=(out, out, out),
        in_specs=[
            pl.BlockSpec((2, step, width), lambda r: (0, r, 0)),
            pl.BlockSpec((step, width), lambda r: (r, 0)),
            pl.BlockSpec((8, HEAD_DIM), lambda r: (0, 0)),
        ],
        out_specs=(row_block,) * 3,
        name="finish",
    )(both, mism, factor)


def solution(mesh):
    rows = P("clip", "blk", None)
    teacher = P(None, ("blk", "clip"), None)
    in_specs = (rows,) * 4 + (teacher,) * 4 + (P(), P(("blk", "clip"), None), P("clip"))
    return jax.shard_map(
        functools.partial(local, mesh.shape["blk"], mesh.shape["clip"]),
        mesh=mesh, in_specs=in_specs, out_specs=(rows,) * 3, check_vma=False,
    )
```

```python
import functools
import math

import jax
import jax.numpy as jnp
from jax import lax
from jax.experimental import pallas as pl
from jax.experimental.pallas import tpu as pltpu
from jax.sharding import PartitionSpec as P

HEAD_DIM = 128
SIGMA = 0.5
OFFSET = 0.1
MESH = pl.DeviceIdType.MESH
F32 = jnp.float32
BF16 = jnp.bfloat16


def kernel(
    nb, nc, hc, chunks,
    slot_ref, token_ref, time_ref,
    q_ref, k_ref, v_ref, res_ref,
    qt_ref, kt_ref, vt_ref, vel_ref,
    both_ref, mism_ref, factor_ref,
    teach, teach_vel, send, recv, stud, dots, own_out, got_out, vel_send, vel_recv, resid, mism, picks,
    part, parts,
    load_sem, send_sem, recv_sem, stud_send, stud_recv, out_send, out_recv,
    vel_ssem, vel_rsem, part_send, part_recv, write_sem,
):
    n = nb * nc
    run = teach.shape[2]
    tok = q_ref.shape[1]
    width = q_ref.shape[2]
    seq = stud.shape[1]
    group_width = width // nb
    cw = hc * HEAD_DIM
    join = 16 // math.gcd(run, 16)
    my_b = lax.axis_index("blk")
    my_c = lax.axis_index("clip")
    me = my_b * nc + my_c

    loads = []
    for t, ref in enumerate((qt_ref, kt_ref, vt_ref)):
        loads.append(pltpu.make_async_copy(ref, teach.at[t], load_sem.at[t]))
    loads.append(pltpu.make_async_copy(vel_ref, teach_vel, load_sem.at[3]))
    loads.append(pltpu.make_async_copy(res_ref.at[0], resid, load_sem.at[4]))
    for load in loads:
        load.start()

    barrier = pltpu.get_barrier_semaphore()

    @pl.loop(1, n)
    def _(m):
        d = lax.rem(me + m, n)
        pl.semaphore_signal(barrier, inc=1, device_id=(d // nc, lax.rem(d, nc)), device_id_type=MESH)

    place = lax.broadcasted_iota(jnp.int32, (1, run), 1)
    for r in range(run):
        picks[r:r + 1, :] = (place == token_ref[0, r]).astype(F32)
    pick = picks[...].astype(BF16)
    time = jnp.full((1, HEAD_DIM), time_ref[0], F32)
    cosine, sine = jnp.cos(time), jnp.sin(time)

    def build(c, d):
        g, i = d // nc, lax.rem(d, nc)
        slot = slot_ref[i]
        col = pl.multiple_of(g * group_width + c * cw, 128)
        pieces = []
        for t in range(3):
            rows = jnp.dot(pick, teach[t, slot, :, pl.ds(col, cw)], preferred_element_type=F32)
            for hh in range(hc):
                pieces.append(rows[:, hh * HEAD_DIM:(hh + 1) * HEAD_DIM])
        spare = send.shape[2] - 3 * hc * run
        if spare:
            pieces.append(jnp.zeros((spare, HEAD_DIM), F32))
        send[c, d] = jnp.concatenate(pieces, axis=0).astype(BF16)

    def students(c):
        for s, ref in enumerate((q_ref, k_ref, v_ref)):
            for off in range(nb):
                g = lax.rem(my_b + off, nb)
                src = ref.at[0, :, pl.ds(pl.multiple_of(g * group_width + c * cw, 128), cw)]
                dst = stud.at[s, pl.ds(pl.multiple_of(my_b * tok, 16), tok), pl.ds(c * cw, cw)]
                if off == 0:
                    pltpu.make_async_copy(src, dst, stud_recv.at[c]).start()
                else:
                    pltpu.make_async_remote_copy(
                        src_ref=src, dst_ref=dst, send_sem=stud_send, recv_sem=stud_recv.at[c],
                        device_id=(g, my_c), device_id_type=MESH,
                    ).start()

    pl.semaphore_wait(barrier, n - 1)
    students(0)
    for load in loads[:3]:
        load.wait()

    for c in range(chunks):
        @pl.loop(1, n)
        def _(m):
            d = lax.rem(my_b + lax.rem(m, nb), nb) * nc + lax.rem(my_c + lax.rem(m // nb * 3, nc), nc)
            build(c, d)
            pltpu.make_async_remote_copy(
                src_ref=send.at[c, d], dst_ref=recv.at[c, me],
                send_sem=send_sem, recv_sem=recv_sem.at[c],
                device_id=(d // nc, lax.rem(d, nc)), device_id_type=MESH,
            ).start()

        build(c, me)
        pltpu.make_async_copy(send.at[c, me], recv.at[c, me], recv_sem.at[c]).start()
        if c > 0:
            students(c)

    loads[3].wait()

    def build_velocity(i):
        slot = slot_ref[i]
        rows = jnp.dot(pick, teach_vel[slot], preferred_element_type=F32)
        heads = [rows[:, h * HEAD_DIM:(h + 1) * HEAD_DIM] for h in range(width // HEAD_DIM)]
        vel_send[i] = jnp.concatenate(heads, axis=0).astype(BF16)

    @pl.loop(1, nc)
    def _(m):
        i = lax.rem(my_c + m, nc)
        build_velocity(i)
        pltpu.make_async_remote_copy(
            src_ref=vel_send.at[i], dst_ref=vel_recv.at[my_c],
            send_sem=vel_ssem, recv_sem=vel_rsem,
            device_id=(my_b, i), device_id_type=MESH,
        ).start()

    build_velocity(my_c)
    pltpu.make_async_copy(vel_send.at[my_c], vel_recv.at[my_c], vel_rsem).start()

    scale = HEAD_DIM ** (-0.5)
    tile = 256
    for c in range(chunks):
        pltpu.make_async_copy(recv.at[c], recv.at[c], recv_sem.at[c]).wait()
        waited = stud.at[:, :, pl.ds(c * cw, cw)]
        pltpu.make_async_copy(waited, waited, stud_recv.at[c]).wait()

        @pl.loop(0, n // join)
        def _(j):
            slabs = [recv[c, j * join + u].astype(F32) for u in range(join)]
            for t in range(3):
                for hh in range(hc):
                    at = (t * hc + hh) * run
                    rows = jnp.concatenate([slab[at:at + run] for slab in slabs], axis=0)
                    dots[t, hh, pl.ds(pl.multiple_of(j * (join * run), 16), join * run), :] = rows.astype(BF16)

        for hh in range(hc):
            lane = c * cw + hh * HEAD_DIM

            @pl.loop(0, seq // tile)
            def _(r):
                at = pl.ds(pl.multiple_of(r * tile, tile), tile)
                keys = stud[1, :, lane:lane + HEAD_DIM]
                both_keys = jnp.concatenate([keys, dots[1, hh]], axis=1)
                both_values = jnp.concatenate([stud[2, :, lane:lane + HEAD_DIM], dots[2, hh]], axis=1)
                query = stud[0, at, lane:lane + HEAD_DIM]
                both_queries = jnp.concatenate([dots[0, hh, at, :], query], axis=1)
                over = (((1,), (1,)), ((), ()))
                scores = lax.dot_general(query, keys, over, preferred_element_type=F32)
                score_dot = lax.dot_general(both_queries, both_keys, over, preferred_element_type=F32)
                top = jnp.max(scores, axis=1, keepdims=True)
                weights = jnp.exp2((scores - top) * (scale * math.log2(math.e)))
                weighted = weights * score_dot
                total = jnp.sum(weights, axis=1, keepdims=True)
                dot_total = jnp.sum(weighted, axis=1, keepdims=True) * scale
                mixed = jnp.dot(weights.astype(BF16), both_values, preferred_element_type=F32)
                carried = jnp.dot(
                    weighted.astype(BF16), both_values[:, :HEAD_DIM], preferred_element_type=F32
                )
                inverse = 1.0 / total
                attention = mixed[:, :HEAD_DIM] * inverse
                tangent = (carried * scale + mixed[:, HEAD_DIM:]) * inverse - (dot_total * inverse) * attention
                own_out[0, at, lane:lane + HEAD_DIM] = attention.astype(BF16)
                own_out[1, at, lane:lane + HEAD_DIM] = tangent.astype(BF16)

        for off in [*range(1, nb), 0]:
            b = lax.rem(my_b + off, nb)
            src = own_out.at[:, pl.ds(pl.multiple_of(b * tok, 16), tok), pl.ds(c * cw, cw)]
            dst = got_out.at[:, :, pl.ds(pl.multiple_of(my_b * group_width + c * cw, 128), cw)]
            if off == 0:
                pltpu.make_async_copy(src, dst, out_recv.at[c]).start()
            else:
                pltpu.make_async_remote_copy(
                    src_ref=src, dst_ref=dst, send_sem=out_send, recv_sem=out_recv.at[c],
                    device_id=(b, my_c), device_id_type=MESH,
                ).start()

    pltpu.make_async_copy(vel_recv, vel_recv, vel_rsem).wait()
    loads[4].wait()
    for c in range(chunks):
        waited = got_out.at[:, :, pl.ds(0, nb * cw)]
        pltpu.make_async_copy(waited, waited, out_recv.at[c]).wait()
    writes = [
        pltpu.make_async_copy(got_out, both_ref, write_sem.at[0]),
        pltpu.make_async_copy(mism, mism_ref, write_sem.at[1]),
    ]
    writes[0].start()

    square_cos, cos_sin = cosine * cosine, cosine * sine
    part[...] = jnp.zeros_like(part)

    @pl.loop(0, width // HEAD_DIM // join)
    def _(j):
        blocks = [
            vel_recv[p, pl.ds(pl.multiple_of(j * (join * run), 16), join * run), :].astype(F32)
            for p in range(nc)
        ]
        added = part[...]
        for u in range(join):
            at = pl.ds(pl.multiple_of((j * join + u) * HEAD_DIM, 128), HEAD_DIM)
            velocity = jnp.concatenate([block[u * run:(u + 1) * run] for block in blocks], axis=0)
            off = -square_cos * (SIGMA * got_out[0, :, at].astype(F32) - velocity) - cos_sin * (
                resid[:, at].astype(F32) + SIGMA * got_out[1, :, at].astype(F32)
            )
            mism[:, at] = off
            added = added + jnp.sum((off * off).reshape(tok // 8, 8, HEAD_DIM), axis=0)
        part[...] = added

    for off in range(1, nb):
        pltpu.make_async_remote_copy(
            src_ref=part, dst_ref=parts.at[off - 1], send_sem=part_send, recv_sem=part_recv,
            device_id=(lax.rem(my_b + off, nb), my_c), device_id_type=MESH,
        ).start()
    writes[1].start()
    pltpu.make_async_copy(parts, parts, part_recv).wait()
    whole = part[...] + jnp.sum(parts[...], axis=0)
    mean_square = jnp.sum(whole, keepdims=True) / (nb * tok * width)
    factor_ref[...] = jnp.broadcast_to(1.0 / (jnp.sqrt(mean_square) + OFFSET), factor_ref.shape)

    pltpu.make_async_copy(parts, parts, part_send).wait()
    sent = recv.at[:, pl.ds(0, n - 1)]
    pltpu.make_async_copy(sent, sent, send_sem).wait()
    sent = stud.at[:, pl.ds(0, (nb - 1) * tok), :]
    pltpu.make_async_copy(sent, sent, stud_send).wait()
    sent = got_out.at[:, :, pl.ds(0, (nb - 1) * group_width)]
    pltpu.make_async_copy(sent, sent, out_send).wait()
    sent = vel_recv.at[pl.ds(0, nc - 1)]
    pltpu.make_async_copy(sent, sent, vel_ssem).wait()
    for write in writes:
        write.wait()


def finish(both_ref, mism_ref, factor_ref, out_ref, tan_ref, target_ref):
    out_ref[0] = both_ref[0]
    tan_ref[0] = both_ref[1]
    target_ref[0] = (mism_ref[...] * factor_ref[0:1, 0:1]).astype(BF16)


def local(
    nb, nc,
    query_rows, key_rows, value_rows, residual,
    query_tangent, key_tangent, value_tangent, velocity,
    clip_slot, token_slot, clip_time,
):
    _, tok, width = query_rows.shape
    clips, run, _ = query_tangent.shape
    n = nb * nc
    seq = nb * tok
    own_heads = width // HEAD_DIM // nb
    hc = 2 if own_heads % 2 == 0 else 1
    chunks = own_heads // hc
    slab = -(-3 * hc * run // 16) * 16
    group_width = width // nb
    heads = width // HEAD_DIM
    out = jax.ShapeDtypeStruct((1, tok, width), BF16)
    anywhere = pl.BlockSpec(memory_space=pl.ANY)
    small = pl.BlockSpec(memory_space=pltpu.SMEM)
    dma = pltpu.SemaphoreType.DMA
    both, mism, factor = pl.pallas_call(
        functools.partial(kernel, nb, nc, hc, chunks),
        out_shape=(
            jax.ShapeDtypeStruct((2, tok, width), BF16),
            jax.ShapeDtypeStruct((tok, width), F32),
            jax.ShapeDtypeStruct((8, HEAD_DIM), F32),
        ),
        in_specs=[small] * 3 + [anywhere] * 8,
        out_specs=(anywhere, anywhere, pl.BlockSpec(memory_space=pltpu.VMEM)),
        scratch_shapes=[
            pltpu.VMEM((3, clips, run, width), BF16),
            pltpu.VMEM((clips, run, width), BF16),
            pltpu.VMEM((chunks, n, slab, HEAD_DIM), BF16),
            pltpu.VMEM((chunks, n, slab, HEAD_DIM), BF16),
            pltpu.VMEM((3, seq, group_width), BF16),
            pltpu.VMEM((3, hc, seq, HEAD_DIM), BF16),
            pltpu.VMEM((2, seq, group_width), BF16),
            pltpu.VMEM((2, tok, width), BF16),
            pltpu.VMEM((nc, heads * run, HEAD_DIM), BF16),
            pltpu.VMEM((nc, heads * run, HEAD_DIM), BF16),
            pltpu.VMEM((tok, width), BF16),
            pltpu.VMEM((tok, width), F32),
            pltpu.VMEM((run, run), F32),
            pltpu.VMEM((8, HEAD_DIM), F32),
            pltpu.VMEM((nb - 1, 8, HEAD_DIM), F32),
            dma((5,)), dma, dma((chunks,)), dma, dma((chunks,)), dma, dma((chunks,)),
            dma, dma, dma, dma, dma((2,)),
        ],
        compiler_params=pltpu.CompilerParams(
            collective_id=0, has_side_effects=True, vmem_limit_bytes=56 * 1024 * 1024
        ),
        name="clip_attention",
    )(
        clip_slot, token_slot, clip_time,
        query_rows, key_rows, value_rows, residual,
        query_tangent, key_tangent, value_tangent, velocity,
    )
    step = tok // 2
    row_block = pl.BlockSpec((1, step, width), lambda r: (0, r, 0))
    return pl.pallas_call(
        finish,
        grid=(tok // step,),
        out_shape=(out, out, out),
        in_specs=[
            pl.BlockSpec((2, step, width), lambda r: (0, r, 0)),
            pl.BlockSpec((step, width), lambda r: (r, 0)),
            pl.BlockSpec((8, HEAD_DIM), lambda r: (0, 0)),
        ],
        out_specs=(row_block,) * 3,
        name="finish",
    )(both, mism, factor)


def solution(mesh):
    rows = P("clip", "blk", None)
    teacher = P(None, ("blk", "clip"), None)
    in_specs = (rows,) * 4 + (teacher,) * 4 + (P(), P(("blk", "clip"), None), P("clip"))
    return jax.shard_map(
        functools.partial(local, mesh.shape["blk"], mesh.shape["clip"]),
        mesh=mesh, in_specs=in_specs, out_specs=(rows,) * 3, check_vma=False,
    )
```
